32 devices in a mesh: grp: 2 (over y), ffn: 4 (over z), wid: 2 (over x), sub: 2 (over core).
Axes of the slice: x: 2, y: 2, z: 4, core: 2. Of those that a mesh axis runs over, the one named last changes fastest.
Arguments:
- states: bfloat16 [2048, 16384], P(('grp', 'ffn'), ('wid', 'sub')), parts along dimension 0
- norm_gain: bfloat16 [16384], P(('wid', 'sub')), may hold values from 0.099609375 to 1.8984375
- query_weight: bfloat16 [16384, 16384], P(('wid', 'sub'), 'ffn')
- key_weight: bfloat16 [16384, 1024], P(('wid', 'sub'), 'ffn')
- value_weight: bfloat16 [16384, 1024], P(('wid', 'sub'), 'ffn'), may hold values from -0.046875 to 0.046875
- output_weight: bfloat16 [16384, 16384], P('ffn', ('wid', 'sub')), may hold values from -0.125 to 0.125
- segments: int32 [2048], P('grp'), parts along dimension 0, may hold values from 0 to 3, never falling along the last dimension, each value on 1 to 512 neighbouring positions
Outputs:
- attention_out: bfloat16 [2048, 16384], P(('grp', 'ffn'), ('wid', 'sub')), parts along dimension 0
The draws below stay inside these ranges and needn't reach their ends.
There are 2 independent parts, one for each index of `grp`. The reference program is written for one: setup_inputs(seed, part) draws one part's arguments, and reference() takes and returns one part's arrays. A program takes and returns all parts, laid end to end along the dimension named above; an argument that names none is the same for every part. Nothing has to cross between parts.
Inputs may be any that keep to these rules, and one draw needn't show every extreme that they name: `segments`: document numbers never fall along the prompt; each of the 4 documents has 1 to 512 tokens, one exactly 512.
All inputs are finite; a program needn't handle non-finite values.
Results may differ from the reference program's by a relative error of at most 0.034.
Values may be sent and summed in bfloat16 or wider, within the bound.
A program may use at most 256 MiB of HBM per device.

```python
import math
import jax
import jax.numpy as jnp
import numpy as np
from jax import lax

D = 16384
HQ = 128
KVH = 8
HD = 128
TOKENS = 1024
DOCS = 4
N_FFN = 4
N_WID = 2
N_SUB = 2


def head_columns(key, heads):
    blocks = jax.vmap(lambda head: jax.random.normal(jax.random.fold_in(key, head), (D, HD), jnp.float32))(heads)
    return jnp.transpose(blocks, (1, 0, 2)).reshape(D, heads.shape[0] * HD)


def draw_states(key, part):
    key = jax.random.fold_in(key, 41)
    row_key, col_key, base_key = jax.random.split(key, 3)
    ramp = 10.0 ** (jnp.arange(D, dtype=jnp.float32) / D)
    rough = jax.random.uniform(col_key, (D,), jnp.float32, 0.5, 2.0)
    rows = 10.0 ** jax.random.uniform(row_key, (TOKENS, 1), jnp.float32)
    base = jax.random.normal(base_key, (TOKENS, D), jnp.float32)
    return (base * rows * (ramp * rough)[None, :]).astype(jnp.bfloat16)


def draw_query_weight(key, part):
    own_key = jax.random.fold_in(key, 17)
    shared = head_columns(key, jnp.arange(HQ, dtype=jnp.int32))
    own = jax.random.normal(own_key, (D, HQ * HD), jnp.float32)
    mixed = (0.9 * shared + 0.44 * own) / math.sqrt(D)
    return mixed.astype(jnp.bfloat16)


def draw_key_weight(key, part):
    own_key = jax.random.fold_in(key, 29)
    own = jax.random.normal(own_key, (D, KVH * HD), jnp.float32) / math.sqrt(D)
    return own.astype(jnp.bfloat16)


def levels(key, dims, shards, least, largest):
    loudness, own = 1.0, jax.random.fold_in(key, 6)
    for axis_at, shards_of in shards:
        draws = jnp.exp(jax.random.uniform(jax.random.fold_in(own, axis_at), (shards_of,), jnp.float32, least / len(shards), largest / len(shards)))
        loudness = loudness * jnp.repeat(draws, dims[axis_at] // shards_of).reshape([-1 if axis == axis_at else 1 for axis in range(len(dims))])
    return loudness


def split_up(count, total, most, skew):
    portions = [(1 << 20) // math.isqrt(standing ** skew) + 1 for standing in range(2, count + 1)]
    rest, given = total - most - (count - 1), [1] * (count - 1)
    while rest > 0:
        movable = [i for i in range(count - 1) if given[i] < most]
        mass, left = sum([portions[i] for i in movable]), rest
        for i in movable:
            more = min(most - given[i], max(1, left * portions[i] // mass), rest)
            given[i] = given[i] + more
            rest = rest - more
    return np.array([most] + given)


def ragged_sizes(rng, count, total, bound, skew):
    if count == 2:
        one = jax.random.randint(rng, (), max(1, total - bound), min(bound, total - 1) + 1)
        return jnp.stack([one, total - one])
    tallies = jnp.asarray(split_up(count, total, bound, skew), jnp.int32)
    couples = (count - 1) // 2
    giver, receiver = tallies[1:1 + 2 * couples:2], tallies[2:2 + 2 * couples:2]
    room = jnp.minimum(giver - 1, bound - receiver)
    shifted = jax.random.randint(jax.random.fold_in(rng, 1), (couples,), 0, 1 << 20) % (room + 1)
    tallies = tallies.at[1:1 + 2 * couples:2].set(giver - shifted).at[2:2 + 2 * couples:2].set(receiver + shifted)
    return tallies[jax.random.permutation(jax.random.fold_in(rng, 2), count)]


def noise(rng, dims, deviation, reach, cuts=(), kind=jnp.bfloat16):
    result = jax.random.normal(rng, dims, jnp.float32) * deviation
    if len(cuts) > 0:
        result = levels(rng, dims, cuts, -0.22, 0.18) * result
    return jnp.clip(result, min=-reach, max=reach).astype(kind)


def setup_inputs(seed: int = 0, part: int = 0) -> dict:
    streams_of = jax.random.split(jax.random.key(seed), 8)
    part_splits = jax.random.split(jax.random.fold_in(streams_of[7], part), 8)
    return {
        "states": draw_states(jax.random.fold_in(jax.random.fold_in(streams_of[7], part), 71), part),
        "norm_gain": jnp.clip(1.0 + 0.18 * jax.random.normal(streams_of[1], (D,), jnp.float32), 0.099609375, 1.8984375).astype(jnp.bfloat16),
        "query_weight": draw_query_weight(jax.random.fold_in(streams_of[7], 71), part),
        "key_weight": draw_key_weight(jax.random.fold_in(streams_of[7], 71), part),
        "value_weight": noise(streams_of[4], (D, KVH * HD), D ** -0.5, 0.046875, ((0, 4), (1, 4))),
        "output_weight": noise(streams_of[5], (HQ * HD, D), (HQ * HD // 8) ** -0.5, 0.125, ((0, 4), (1, 4))),
        "segments": jnp.searchsorted(jnp.cumsum(ragged_sizes(part_splits[6], DOCS, TOKENS, TOKENS // 2, 1)), jnp.arange(TOKENS), side="right").astype(jnp.int32),
    }


EPS = 1e-05
THETA = 500000.0
NEGATIVE = -1e+30

def rope_tables(positions):
    half = HD // 2
    freqs = THETA ** (-(jnp.arange(half, dtype=jnp.float32) * 2.0 / HD))
    angles = positions.astype(jnp.float32)[:, None] * freqs[None, :]
    return (jnp.cos(angles), jnp.sin(angles))

def rotate(tensor, cosine, sine):
    half = HD // 2
    first = tensor[..., :half]
    second = tensor[..., half:]
    cosine = cosine[:, None, :]
    sine = sine[:, None, :]
    return jnp.concatenate([first * cosine - second * sine, second * cosine + first * sine], axis=-1)

def blocked_product(left, right, pieces):
    inner = left.shape[1] // pieces

    def one_piece(total, index):
        start = (index * inner).astype(jnp.int32)
        left_part = lax.dynamic_slice_in_dim(left, start, inner, 1)
        right_part = lax.dynamic_slice_in_dim(right, start, inner, 0)
        term = jnp.dot(left_part, right_part, preferred_element_type=jnp.float32).astype(jnp.bfloat16)
        term = lax.optimization_barrier(term)
        return (total + term.astype(jnp.float32), None)
    empty = jnp.zeros((left.shape[0], right.shape[1]), jnp.float32)
    total, _ = lax.scan(one_piece, empty, jnp.arange(pieces, dtype=jnp.int32))
    return total

def reference(states, norm_gain, query_weight, key_weight, value_weight, output_weight, segments):
    wide_states = states.astype(jnp.float32)
    scaling = lax.rsqrt(lax.optimization_barrier(jnp.mean(wide_states * wide_states, axis=1, keepdims=True)) + EPS)
    normed = (wide_states * scaling * norm_gain.astype(jnp.float32)[None, :]).astype(jnp.bfloat16)
    width_pieces = N_WID * N_SUB
    query_sum = blocked_product(normed, query_weight, width_pieces)
    key_sum = blocked_product(normed, key_weight, width_pieces)
    value_sum = blocked_product(normed, value_weight, width_pieces)
    positions = jnp.arange(TOKENS, dtype=jnp.int32)
    cosine, sine = rope_tables(positions)
    queries = (rotate(query_sum.reshape(TOKENS, HQ, HD), cosine, sine) * HD ** (-0.5)).astype(jnp.bfloat16)
    keys = rotate(key_sum.reshape(TOKENS, KVH, HD), cosine, sine).astype(jnp.bfloat16)
    values = value_sum.reshape(TOKENS, KVH, HD).astype(jnp.bfloat16)
    group = HQ // KVH
    grouped = queries.reshape(TOKENS, KVH, group, HD)
    allowed = (segments[:, None] == segments[None, :]) & (positions[None, :] <= positions[:, None])

    def one_head(index):
        query_part = lax.dynamic_index_in_dim(grouped, index, 1, keepdims=False).astype(jnp.float32)
        key_part = lax.dynamic_index_in_dim(keys, index, 1, keepdims=False).astype(jnp.float32)
        value_part = lax.dynamic_index_in_dim(values, index, 1, keepdims=False).astype(jnp.float32)
        scores = jnp.einsum('tgd,sd->gts', query_part, key_part)
        masked = jnp.where(allowed[None], scores, NEGATIVE)
        highest = lax.optimization_barrier(jnp.max(masked, axis=-1, keepdims=True))
        weights = jnp.exp(masked - highest)
        total = lax.optimization_barrier(jnp.sum(weights, axis=-1, keepdims=True))
        probs = (weights / total).astype(jnp.bfloat16)
        return jnp.einsum('gts,sd->tgd', probs.astype(jnp.float32), value_part).astype(jnp.bfloat16)
    mixed = lax.map(one_head, jnp.arange(KVH, dtype=jnp.int32))
    attended = jnp.transpose(mixed, (1, 0, 2, 3)).reshape(TOKENS, HQ * HD)
    return blocked_product(attended, output_weight, N_FFN).astype(jnp.bfloat16)
```

```python
import jax
import jax.numpy as jnp
import numpy as np
from jax import lax
from jax.sharding import PartitionSpec as P

KVH = 8
HD = 128


EPS = 1e-05
THETA = 500000.0
NEGATIVE = -1e30
CHAINS = 2


def swapped(value, axis, distance):
    mask = 2**distance
    pairs = [(source, source ^ mask) for source in range(lax.axis_size(axis))]
    return lax.ppermute(value, axis, pairs)


def rope_tables(positions):
    half = HD // 2
    freqs = THETA ** (-(jnp.arange(half, dtype=jnp.float32) * 2.0 / HD))
    angles = positions.astype(jnp.float32)[:, None] * freqs[None, :]
    return (jnp.cos(angles), jnp.sin(angles))


def rotate(tensor, cosine, sine):
    half = HD // 2
    first = tensor[..., :half]
    second = tensor[..., half:]
    cosine = cosine[:, None, :]
    sine = sine[:, None, :]
    return jnp.concatenate(
        [first * cosine - second * sine, second * cosine + first * sine], axis=-1
    )


def block_orders(count):
    return np.array(
        [sorted(range(count), key=lambda b: (abs(b - z), b)) for z in range(count)], dtype=np.int32
    )


def pick(choices, wanted, place):
    used = sorted({w for w in wanted if w is not None})
    result = choices[used[0]]
    for option in used[1:]:
        table = jnp.asarray(np.array([w == option for w in wanted]))
        result = jnp.where(table[place], choices[option], result)
    return result


def body(states, norm_gain, query_weight, key_weight, value_weight, output_weight, segments):
    n = lax.axis_size("ffn")
    place = lax.axis_index("ffn")
    inner = lax.axis_size(("wid", "sub"))
    inner_at = lax.axis_index(("wid", "sub"))
    orders = block_orders(n)
    slots = np.argsort(orders, axis=1)
    rows = states.shape[0]
    total_rows = rows * n
    query_cols = query_weight.shape[1]
    key_cols = key_weight.shape[1]

    from_below, from_above = {0: states}, {0: states}
    for s in range(1, n):
        from_below[s] = lax.ppermute(
            from_below[s - 1], "ffn", [(i, i + 1) for i in range(s - 1, n - 1)]
        )
        from_above[s] = lax.ppermute(
            from_above[s - 1], "ffn", [(i, i - 1) for i in range(1, n - s + 1)]
        )
    arrived = {}
    for s in range(n):
        arrived[s], arrived[-s] = from_above[s], from_below[s]

    wide_states = states.astype(jnp.float32)
    width = states.shape[1] * inner
    square_sum = lax.psum(jnp.sum(wide_states * wide_states, axis=1), ("wid", "sub"))
    own_scaling = lax.rsqrt(square_sum / width + EPS)
    all_scaling = lax.all_gather(own_scaling, "ffn", axis=0, tiled=False)
    gain = norm_gain.astype(jnp.float32)[None, :]

    order_here = jnp.asarray(orders)[place]
    query_rows = rows // inner
    slot_queries, slot_kv, slot_row_ids, slot_products = [], [], [], []
    heads_here = query_cols // HD
    for slot in range(n):
        block = order_here[slot]
        steps = [int(orders[z][slot]) - z for z in range(n)]
        choices = {step: arrived[step] for step in sorted(set(steps))}
        if slot > 0:
            choices, _ = lax.optimization_barrier((choices, query_part))
        piece = pick(choices, steps, place)
        scaling = lax.dynamic_index_in_dim(all_scaling, block, 0, keepdims=False)[:, None]
        normed = (piece.astype(jnp.float32) * scaling * gain).astype(jnp.bfloat16)
        kv_part = jnp.stack(
            [
                jnp.dot(normed, key_weight, preferred_element_type=jnp.float32).astype(jnp.bfloat16),
                jnp.dot(normed, value_weight, preferred_element_type=jnp.float32).astype(jnp.bfloat16),
            ]
        )
        if slot > 0:
            kv_part, slot_kv[-1] = lax.optimization_barrier((kv_part, slot_kv[-1]))
        slot_kv.append(lax.psum(kv_part, ("wid", "sub")))
        query_part = jnp.dot(normed, query_weight, preferred_element_type=jnp.float32).astype(
            jnp.bfloat16
        )
        slot_products.append(query_part)

    for slot in range(n):
        block = order_here[slot]
        query_sum = lax.psum_scatter(
            slot_products[slot], ("wid", "sub"), scatter_dimension=0, tiled=True
        ).astype(jnp.float32)
        row_ids = block * rows + inner_at * query_rows + jnp.arange(query_rows, dtype=jnp.int32)
        query_cos, query_sin = rope_tables(row_ids)
        queries = (
            rotate(query_sum.reshape(query_rows, heads_here, HD), query_cos, query_sin)
            * HD ** (-0.5)
        ).astype(jnp.bfloat16)
        slot_queries.append(queries)
        slot_row_ids.append(row_ids)

    stacked = jnp.stack(slot_kv)
    slot_of = jnp.asarray(slots.astype(np.int32))[place]
    kv_stack = jnp.concatenate(
        [lax.dynamic_index_in_dim(stacked, slot_of[b], 0, keepdims=False) for b in range(n)], axis=1
    )
    reach = max(1, n // KVH)
    for bit_number in range(reach.bit_length() - 1):
        partner = swapped(kv_stack, "ffn", bit_number)
        lower = place // 2**bit_number % 2 == 0
        kv_stack = jnp.where(
            lower,
            jnp.concatenate([kv_stack, partner], axis=2),
            jnp.concatenate([partner, kv_stack], axis=2),
        )
    kv_heads = kv_stack.shape[2] // HD
    per_group = heads_here // kv_heads
    all_rows = jnp.arange(total_rows, dtype=jnp.int32)
    cosine, sine = rope_tables(all_rows)
    keys = rotate(
        kv_stack[0].astype(jnp.float32).reshape(total_rows, kv_heads, HD), cosine, sine
    ).astype(jnp.bfloat16)
    values = kv_stack[1].reshape(total_rows, kv_heads, HD)

    def attend(queries, row_ids):
        queries = queries.reshape(query_rows, kv_heads, per_group, HD)
        query_segments = lax.dynamic_slice_in_dim(segments, row_ids[0], query_rows)
        allowed = (query_segments[:, None] == segments[None, :]) & (
            all_rows[None, :] <= row_ids[:, None]
        )
        scores = jnp.einsum("tcpd,scd->cpts", queries, keys, preferred_element_type=jnp.float32)
        masked = jnp.where(allowed[None, None], scores, NEGATIVE)
        highest = jnp.max(masked, axis=-1, keepdims=True)
        weights = jnp.exp(masked - highest)
        total = jnp.sum(weights, axis=-1, keepdims=True)
        probs = (weights / total).astype(jnp.bfloat16)
        result = jnp.einsum("cpts,scd->tcpd", probs, values, preferred_element_type=jnp.float32)
        return result.astype(jnp.bfloat16).reshape(query_rows, heads_here * HD)

    terms = [None] * n
    for slot in reversed(range(n)):
        attended = attend(slot_queries[slot], slot_row_ids[slot])
        terms[slot] = jnp.dot(
            lax.all_gather(attended, ("wid", "sub"), axis=0, tiled=True),
            output_weight,
            preferred_element_type=jnp.float32,
        ).astype(jnp.bfloat16)

    cols = output_weight.shape[1]
    outs = []
    for chain in range(CHAINS):
        part = [t[:, chain * cols // CHAINS : (chain + 1) * cols // CHAINS] for t in terms]
        below = above = None
        for r in range(n - 1, 0, -1):
            up_wanted = [int(slots[z][z + r]) if z + r < n else None for z in range(n)]
            down_wanted = [int(slots[z][z - r]) if z - r >= 0 else None for z in range(n)]
            up = pick(part, up_wanted, place)
            down = pick(part, down_wanted, place)
            if below is not None:
                up = (up.astype(jnp.float32) + below.astype(jnp.float32)).astype(jnp.bfloat16)
                down = (down.astype(jnp.float32) + above.astype(jnp.float32)).astype(jnp.bfloat16)
            below = lax.ppermute(up, "ffn", [(i, i + 1) for i in range(n - r)])
            above = lax.ppermute(down, "ffn", [(i, i - 1) for i in range(r, n)])
        total = part[0].astype(jnp.float32)
        if below is not None:
            total = total + below.astype(jnp.float32) + above.astype(jnp.float32)
        outs.append(total.astype(jnp.bfloat16))
    return jnp.concatenate(outs, axis=1)


def solution(mesh):
    in_specs = (
        P(("grp", "ffn"), ("wid", "sub")),
        P(("wid", "sub")),
        P(("wid", "sub"), "ffn"),
        P(("wid", "sub"), "ffn"),
        P(("wid", "sub"), "ffn"),
        P("ffn", ("wid", "sub")),
        P("grp"),
    )
    out_specs = P(("grp", "ffn"), ("wid", "sub"))
    return jax.shard_map(body, mesh=mesh, in_specs=in_specs, out_specs=out_specs, check_vma=False)
```

```python
import jax
import jax.numpy as jnp
import numpy as np
from jax import lax
from jax.sharding import PartitionSpec as P

KVH = 8
HD = 128


EPS = 1e-05
THETA = 500000.0
NEGATIVE = -1e30
CHAINS = 2


def swapped(value, axis, distance):
    mask = 2**distance
    pairs = [(source, source ^ mask) for source in range(lax.axis_size(axis))]
    return lax.ppermute(value, axis, pairs)


def rope_tables(positions):
    half = HD // 2
    freqs = THETA ** (-(jnp.arange(half, dtype=jnp.float32) * 2.0 / HD))
    angles = positions.astype(jnp.float32)[:, None] * freqs[None, :]
    return (jnp.cos(angles), jnp.sin(angles))


def rotate(tensor, cosine, sine):
    half = HD // 2
    first = tensor[..., :half]
    second = tensor[..., half:]
    cosine = cosine[:, None, :]
    sine = sine[:, None, :]
    return jnp.concatenate(
        [first * cosine - second * sine, second * cosine + first * sine], axis=-1
    )


def block_orders(count):
    return np.array(
        [sorted(range(count), key=lambda b: (abs(b - z), b)) for z in range(count)], dtype=np.int32
    )


def pick(choices, wanted, place):
    used = sorted({w for w in wanted if w is not None})
    result = choices[used[0]]
    for option in used[1:]:
        table = jnp.asarray(np.array([w == option for w in wanted]))
        result = jnp.where(table[place], choices[option], result)
    return result


def added(left, right):
    return (left.astype(jnp.float32) + right.astype(jnp.float32)).astype(jnp.bfloat16)


def inner_stages():
    return [
        (axis, bit)
        for axis in ("sub", "wid")
        for bit in range(lax.axis_size(axis).bit_length() - 1)
    ]


def bit_of(axis, bit):
    return lax.axis_index(axis) // 2**bit % 2


def summed(value, stages):
    for axis, bit in stages:
        value = added(value, swapped(value, axis, bit))
    return value


def scattered_sum(value, stages):
    first = 0
    for axis, bit in stages:
        half = value.shape[0] // 2
        upper = bit_of(axis, bit) == 1
        low, high = value[:half], value[half:]
        value = added(
            jnp.where(upper, high, low), swapped(jnp.where(upper, low, high), axis, bit)
        )
        first = first + bit_of(axis, bit) * half
    return value, first


def gathered(value, stages):
    for axis, bit in reversed(stages):
        other = swapped(value, axis, bit)
        upper = bit_of(axis, bit) == 1
        value = jnp.concatenate(
            [jnp.where(upper, other, value), jnp.where(upper, value, other)], axis=0
        )
    return value


def body(states, norm_gain, query_weight, key_weight, value_weight, output_weight, segments):
    n = lax.axis_size("ffn")
    place = lax.axis_index("ffn")
    inner = lax.axis_size(("wid", "sub"))
    orders = block_orders(n)
    slots = np.argsort(orders, axis=1)
    rows = states.shape[0]
    total_rows = rows * n
    query_cols = query_weight.shape[1]
    key_cols = key_weight.shape[1]

    wide_states = states.astype(jnp.float32)
    width = states.shape[1] * inner
    square_sum = lax.psum(jnp.sum(wide_states * wide_states, axis=1), ("wid", "sub"))
    scaling = lax.rsqrt(square_sum[:, None] / width + EPS)
    normed = (wide_states * scaling * norm_gain.astype(jnp.float32)[None, :]).astype(jnp.bfloat16)

    arrived = {0: normed}
    for s in range(1, n):
        arrived[-s] = lax.ppermute(arrived[1 - s], "ffn", [(i, i + 1) for i in range(s - 1, n - 1)])
        arrived[s] = lax.ppermute(arrived[s - 1], "ffn", [(i, i - 1) for i in range(1, n - s + 1)])

    order_here = jnp.asarray(orders)[place]
    query_rows = rows // inner
    slot_kv, slot_products = [], []
    heads_here = query_cols // HD
    stages = inner_stages()
    for slot in range(n):
        steps = [int(orders[z][slot]) - z for z in range(n)]
        choices = {step: arrived[step] for step in sorted(set(steps))}
        if slot > 0:
            choices, _ = lax.optimization_barrier((choices, query_part))
        piece = pick(choices, steps, place)
        kv_part = jnp.concatenate(
            [
                jnp.dot(piece, key_weight, preferred_element_type=jnp.float32),
                jnp.dot(piece, value_weight, preferred_element_type=jnp.float32),
            ],
            axis=1,
        ).astype(jnp.bfloat16)
        slot_kv.append(summed(kv_part, stages))
        query_part = jnp.dot(piece, query_weight, preferred_element_type=jnp.float32).astype(
            jnp.bfloat16
        )
        slot_products.append(query_part)

    slot_queries, slot_row_ids = [], []
    for slot in range(n):
        query_sum, first = scattered_sum(slot_products[slot], stages)
        row_ids = order_here[slot] * rows + first + jnp.arange(query_rows, dtype=jnp.int32)
        query_cos, query_sin = rope_tables(row_ids)
        queries = (
            rotate(
                query_sum.astype(jnp.float32).reshape(query_rows, heads_here, HD),
                query_cos,
                query_sin,
            )
            * HD ** (-0.5)
        ).astype(jnp.bfloat16)
        slot_queries.append(queries)
        slot_row_ids.append(row_ids)

    stacked = jnp.stack(slot_kv)
    slot_of = jnp.asarray(slots.astype(np.int32))[place]
    kv_stack = jnp.concatenate(
        [lax.dynamic_index_in_dim(stacked, slot_of[b], 0, keepdims=False) for b in range(n)], axis=0
    )
    kv_stack = jnp.stack([kv_stack[:, :key_cols], kv_stack[:, key_cols:]])
    reach = max(1, n // KVH)
    for bit_number in range(reach.bit_length() - 1):
        partner = swapped(kv_stack, "ffn", bit_number)
        lower = place // 2**bit_number % 2 == 0
        kv_stack = jnp.where(
            lower,
            jnp.concatenate([kv_stack, partner], axis=2),
            jnp.concatenate([partner, kv_stack], axis=2),
        )
    kv_heads = kv_stack.shape[2] // HD
    per_group = heads_here // kv_heads
    all_rows = jnp.arange(total_rows, dtype=jnp.int32)
    cosine, sine = rope_tables(all_rows)
    keys = rotate(
        kv_stack[0].astype(jnp.float32).reshape(total_rows, kv_heads, HD), cosine, sine
    ).astype(jnp.bfloat16)
    values = kv_stack[1].reshape(total_rows, kv_heads, HD)

    def attend(queries, row_ids):
        queries = queries.reshape(query_rows, kv_heads, per_group, HD)
        query_segments = lax.dynamic_slice_in_dim(segments, row_ids[0], query_rows)
        allowed = (query_segments[:, None] == segments[None, :]) & (
            all_rows[None, :] <= row_ids[:, None]
        )
        scores = jnp.einsum("tcpd,scd->cpts", queries, keys, preferred_element_type=jnp.float32)
        masked = jnp.where(allowed[None, None], scores, NEGATIVE)
        highest = jnp.max(masked, axis=-1, keepdims=True)
        weights = jnp.exp(masked - highest)
        total = jnp.sum(weights, axis=-1, keepdims=True)
        probs = (weights / total).astype(jnp.bfloat16)
        result = jnp.einsum("cpts,scd->tcpd", probs, values, preferred_element_type=jnp.float32)
        return result.astype(jnp.bfloat16).reshape(query_rows, heads_here * HD)

    cols = output_weight.shape[1]
    width_of = cols // CHAINS
    parts = [[None] * n for _ in range(CHAINS)]
    for slot in reversed(range(n)):
        attended = gathered(attend(slot_queries[slot], slot_row_ids[slot]), stages)
        for chain in range(CHAINS):
            parts[chain][slot] = jnp.dot(
                attended,
                output_weight[:, chain * width_of : (chain + 1) * width_of],
                preferred_element_type=jnp.float32,
            ).astype(jnp.bfloat16)

    taken = [None] * CHAINS
    sent = None
    for r in range(n - 1, 0, -1):
        up_wanted = [int(slots[z][z + r]) if z + r < n else None for z in range(n)]
        down_wanted = [int(slots[z][z - r]) if z - r >= 0 else None for z in range(n)]
        for chain in range(CHAINS):
            got = taken[chain]
            if sent is not None and got is not None:
                got, _ = lax.optimization_barrier((got, sent))
            up = pick(parts[chain], up_wanted, place)
            down = pick(parts[chain], down_wanted, place)
            if got is not None:
                up = added(up, got[0])
                down = added(down, got[1])
            sent = (up, down)
            taken[chain] = (
                lax.ppermute(up, "ffn", [(i, i + 1) for i in range(n - r)]),
                lax.ppermute(down, "ffn", [(i, i - 1) for i in range(r, n)]),
            )
    outs = []
    for chain in range(CHAINS):
        total = parts[chain][0].astype(jnp.float32)
        if taken[chain] is not None:
            below, above = taken[chain]
            total = total + below.astype(jnp.float32) + above.astype(jnp.float32)
        outs.append(total.astype(jnp.bfloat16))
    return jnp.concatenate(outs, axis=1)


def solution(mesh):
    in_specs = (
        P(("grp", "ffn"), ("wid", "sub")),
        P(("wid", "sub")),
        P(("wid", "sub"), "ffn"),
        P(("wid", "sub"), "ffn"),
        P(("wid", "sub"), "ffn"),
        P("ffn", ("wid", "sub")),
        P("grp"),
    )
    out_specs = P(("grp", "ffn"), ("wid", "sub"))
    return jax.shard_map(body, mesh=mesh, in_specs=in_specs, out_specs=out_specs, check_vma=False)
```

```python
import jax
import jax.numpy as jnp
import numpy as np
from jax import lax
from jax.sharding import PartitionSpec as P

KVH = 8
HD = 128


EPS = 1e-05
THETA = 500000.0
NEGATIVE = -1e30
CHAINS = 2


def swapped(value, axis, distance):
    mask = 2**distance
    pairs = [(source, source ^ mask) for source in range(lax.axis_size(axis))]
    return lax.ppermute(value, axis, pairs)


def rope_tables(positions):
    half = HD // 2
    freqs = THETA ** (-(jnp.arange(half, dtype=jnp.float32) * 2.0 / HD))
    angles = positions.astype(jnp.float32)[:, None] * freqs[None, :]
    return (jnp.cos(angles), jnp.sin(angles))


def rotate(tensor, cosine, sine):
    half = HD // 2
    first = tensor[..., :half]
    second = tensor[..., half:]
    cosine = cosine[:, None, :]
    sine = sine[:, None, :]
    return jnp.concatenate(
        [first * cosine - second * sine, second * cosine + first * sine], axis=-1
    )


def block_orders(count):
    return np.array(
        [sorted(range(count), key=lambda b: (abs(b - z), b)) for z in range(count)], dtype=np.int32
    )


def pick(choices, wanted, place):
    used = sorted({w for w in wanted if w is not None})
    result = choices[used[0]]
    for option in used[1:]:
        table = jnp.asarray(np.array([w == option for w in wanted]))
        result = jnp.where(table[place], choices[option], result)
    return result


def added(left, right):
    return (left.astype(jnp.float32) + right.astype(jnp.float32)).astype(jnp.bfloat16)


def inner_stages():
    return [
        (axis, bit)
        for axis in ("sub", "wid")
        for bit in range(lax.axis_size(axis).bit_length() - 1)
    ]


def bit_of(axis, bit):
    return lax.axis_index(axis) // 2**bit % 2


def summed(value, stages):
    for axis, bit in stages:
        value = added(value, swapped(value, axis, bit))
    return value


def scattered_sum(value, stages):
    first = 0
    for axis, bit in stages:
        half = value.shape[0] // 2
        upper = bit_of(axis, bit) == 1
        low, high = value[:half], value[half:]
        value = added(
            jnp.where(upper, high, low), swapped(jnp.where(upper, low, high), axis, bit)
        )
        first = first + bit_of(axis, bit) * half
    return value, first


def gathered(value, stages):
    for axis, bit in reversed(stages):
        other = swapped(value, axis, bit)
        upper = bit_of(axis, bit) == 1
        value = jnp.concatenate(
            [jnp.where(upper, other, value), jnp.where(upper, value, other)], axis=0
        )
    return value


def body(states, norm_gain, query_weight, key_weight, value_weight, output_weight, segments):
    n = lax.axis_size("ffn")
    place = lax.axis_index("ffn")
    inner = lax.axis_size(("wid", "sub"))
    orders = block_orders(n)
    slots = np.argsort(orders, axis=1)
    rows = states.shape[0]
    total_rows = rows * n
    query_cols = query_weight.shape[1]
    key_cols = key_weight.shape[1]

    wide_states = states.astype(jnp.float32)
    width = states.shape[1] * inner
    square_sum = lax.psum(jnp.sum(wide_states * wide_states, axis=1), ("wid", "sub"))
    scaling = lax.rsqrt(square_sum[:, None] / width + EPS)
    normed = (wide_states * scaling * norm_gain.astype(jnp.float32)[None, :]).astype(jnp.bfloat16)

    arrived = {0: normed}
    for s in range(1, n):
        arrived[-s] = lax.ppermute(arrived[1 - s], "ffn", [(i, i + 1) for i in range(s - 1, n - 1)])
        arrived[s] = lax.ppermute(arrived[s - 1], "ffn", [(i, i - 1) for i in range(1, n - s + 1)])

    order_here = jnp.asarray(orders)[place]
    query_rows = rows // inner
    slot_kv, slot_products = [], []
    heads_here = query_cols // HD
    stages = inner_stages()
    for slot in range(n):
        steps = [int(orders[z][slot]) - z for z in range(n)]
        choices = {step: arrived[step] for step in sorted(set(steps))}
        if slot > 0:
            choices, _ = lax.optimization_barrier((choices, query_part))
        piece = pick(choices, steps, place)
        kv_part = jnp.concatenate(
            [
                jnp.dot(piece, key_weight, preferred_element_type=jnp.float32),
                jnp.dot(piece, value_weight, preferred_element_type=jnp.float32),
            ],
            axis=1,
        ).astype(jnp.bfloat16)
        slot_kv.append(summed(kv_part, stages))
        query_part = jnp.dot(piece, query_weight, preferred_element_type=jnp.float32).astype(
            jnp.bfloat16
        )
        slot_products.append(query_part)

    slot_queries, slot_row_ids = [], []
    for slot in range(n):
        query_sum, first = scattered_sum(slot_products[slot], stages)
        row_ids = order_here[slot] * rows + first + jnp.arange(query_rows, dtype=jnp.int32)
        query_cos, query_sin = rope_tables(row_ids)
        queries = (
            rotate(
                query_sum.astype(jnp.float32).reshape(query_rows, heads_here, HD),
                query_cos,
                query_sin,
            )
            * HD ** (-0.5)
        ).astype(jnp.bfloat16)
        slot_queries.append(queries)
        slot_row_ids.append(row_ids)

    stacked = jnp.stack(slot_kv)
    slot_of = jnp.asarray(slots.astype(np.int32))[place]
    kv_stack = jnp.concatenate(
        [lax.dynamic_index_in_dim(stacked, slot_of[b], 0, keepdims=False) for b in range(n)], axis=0
    )
    kv_stack = jnp.stack([kv_stack[:, :key_cols], kv_stack[:, key_cols:]])
    reach = max(1, n // KVH)
    for bit_number in range(reach.bit_length() - 1):
        partner = swapped(kv_stack, "ffn", bit_number)
        lower = place // 2**bit_number % 2 == 0
        kv_stack = jnp.where(
            lower,
            jnp.concatenate([kv_stack, partner], axis=2),
            jnp.concatenate([partner, kv_stack], axis=2),
        )
    kv_heads = kv_stack.shape[2] // HD
    per_group = heads_here // kv_heads
    all_rows = jnp.arange(total_rows, dtype=jnp.int32)
    cosine, sine = rope_tables(all_rows)
    keys = rotate(
        kv_stack[0].astype(jnp.float32).reshape(total_rows, kv_heads, HD), cosine, sine
    ).astype(jnp.bfloat16)
    values = kv_stack[1].reshape(total_rows, kv_heads, HD)

    def attend(queries, row_ids):
        queries = queries.reshape(query_rows, kv_heads, per_group, HD)
        query_segments = lax.dynamic_slice_in_dim(segments, row_ids[0], query_rows)
        allowed = (query_segments[:, None] == segments[None, :]) & (
            all_rows[None, :] <= row_ids[:, None]
        )
        scores = jnp.einsum("tcpd,scd->cpts", queries, keys, preferred_element_type=jnp.float32)
        masked = jnp.where(allowed[None, None], scores, NEGATIVE)
        highest = jnp.max(masked, axis=-1, keepdims=True)
        weights = jnp.exp(masked - highest)
        total = jnp.sum(weights, axis=-1, keepdims=True)
        probs = (weights / total).astype(jnp.bfloat16)
        result = jnp.einsum("cpts,scd->tcpd", probs, values, preferred_element_type=jnp.float32)
        return result.astype(jnp.bfloat16).reshape(query_rows, heads_here * HD)

    cols = output_weight.shape[1]
    width_of = cols // CHAINS
    parts = [[None] * n for _ in range(CHAINS)]
    own_rows, terms = [None] * n, [None] * n
    for slot in reversed(range(n)):
        queries = slot_queries[slot]
        if slot + 1 < n:
            queries, _ = lax.optimization_barrier((queries, own_rows[slot + 1]))
        if slot + 2 < n:
            queries, _ = lax.optimization_barrier((queries, terms[slot + 2]))
        own_rows[slot] = attend(queries, slot_row_ids[slot])
        terms[slot] = jnp.dot(
            gathered(own_rows[slot], stages), output_weight, preferred_element_type=jnp.float32
        ).astype(jnp.bfloat16)
        for chain in range(CHAINS):
            parts[chain][slot] = terms[slot][:, chain * width_of : (chain + 1) * width_of]

    taken = [None] * CHAINS
    sent = None
    for r in range(n - 1, 0, -1):
        up_wanted = [int(slots[z][z + r]) if z + r < n else None for z in range(n)]
        down_wanted = [int(slots[z][z - r]) if z - r >= 0 else None for z in range(n)]
        for chain in range(CHAINS):
            got = taken[chain]
            if sent is not None and got is not None:
                got, _ = lax.optimization_barrier((got, sent))
            up = pick(parts[chain], up_wanted, place)
            down = pick(parts[chain], down_wanted, place)
            if got is not None:
                up = added(up, got[0])
                down = added(down, got[1])
            sent = (up, down)
            taken[chain] = (
                lax.ppermute(up, "ffn", [(i, i + 1) for i in range(n - r)]),
                lax.ppermute(down, "ffn", [(i, i - 1) for i in range(r, n)]),
            )
    outs = []
    for chain in range(CHAINS):
        total = parts[chain][0].astype(jnp.float32)
        if taken[chain] is not None:
            below, above = taken[chain]
            total = total + below.astype(jnp.float32) + above.astype(jnp.float32)
        outs.append(total.astype(jnp.bfloat16))
    return jnp.concatenate(outs, axis=1)


def solution(mesh):
    in_specs = (
        P(("grp", "ffn"), ("wid", "sub")),
        P(("wid", "sub")),
        P(("wid", "sub"), "ffn"),
        P(("wid", "sub"), "ffn"),
        P(("wid", "sub"), "ffn"),
        P("ffn", ("wid", "sub")),
        P("grp"),
    )
    out_specs = P(("grp", "ffn"), ("wid", "sub"))
    return jax.shard_map(body, mesh=mesh, in_specs=in_specs, out_specs=out_specs, check_vma=False)
```
